128 devices in a mesh: ctx: 16 (over x_hi, z, core), tp: 8 (over y, x_lo).
Axes of the slice: x: 4 (x_hi: 2, x_lo: 2; x = x_hi * 2 + x_lo), y: 4, z: 4, core: 2. Of those that a mesh axis runs over, the one named last changes fastest.
Arguments:
- queries: bfloat16 [4, 128, 128, 128], P(None, ('ctx', 'tp')), may hold values from -6.5 to 6.5
- new_keys: bfloat16 [4, 128, 8, 128], P(None, ('ctx', 'tp')), may hold values from -4 to 4
- turn_value_rows: bfloat16 [4, 128, 8, 128], P(None, ('ctx', 'tp')), may hold values from -4 to 4
- cache_keys: bfloat16 [4, 32768, 8, 128], P(None, 'ctx', 'tp'), may hold values from -4 to 4
- cache_values: bfloat16 [4, 32768, 8, 128], P(None, 'ctx', 'tp'), may hold values from -4 to 4
- cached_len: int32 [4], replicated, may hold values from 1 to 32768, 81920 in all
- new_len: int32 [4], replicated, may hold values from 1 to 128, as said below
- fold: int32 [16], replicated, may hold values from 0 to 15, each once
Outputs:
- attended: bfloat16 [4, 128, 128, 128], P(None, ('ctx', 'tp'))
The draws below stay inside these ranges and needn't reach their ends.
Inputs may be any that keep to these rules, and one draw needn't show every extreme that they name: `cached_len`: one rollout has a full cache. `new_len`: one rollout fills all 128 slots. `fold`: a permutation of the storage blocks.
All inputs are finite; a program needn't handle non-finite values.
Results may differ from the reference program's by a relative error of at most 0.025.
Values may be sent and summed in bfloat16 or wider, within the bound.
A program may use at most 128 MiB of HBM per device.

```python
import math
import jax
import jax.numpy as jnp
import numpy as np
from jax import lax

HD = 128
GROUP = 16
ROLLOUTS = 4
CACHE_DEV = 2048
KVH = 8
H = 128
CACHE = 32768
NEW = 128
SHARDS = 16


def draw_queries(key, part):
    key = jax.random.fold_in(key, 1)
    values = jnp.clip(jax.random.normal(key, (ROLLOUTS, NEW, H, HD), jnp.float32), -4.0, 4.0)
    return values.astype(jnp.bfloat16)


def draw_cache_keys(key, part):
    key = jax.random.fold_in(key, 2)
    values = jnp.clip(jax.random.normal(key, (ROLLOUTS, CACHE, KVH, HD), jnp.float32), -4.0, 4.0)
    return values.astype(jnp.bfloat16)


def draw_new_len(key, part):
    key = jax.random.fold_in(key, 3)
    dispersion = jax.random.randint(jax.random.fold_in(key, 1), (ROLLOUTS,), 1, NEW + 1, dtype=jnp.int32)
    full_one = jax.random.randint(jax.random.fold_in(key, 2), (), 0, ROLLOUTS, dtype=jnp.int32)
    return jnp.where(jnp.arange(ROLLOUTS, dtype=jnp.int32) == full_one, NEW, dispersion).astype(jnp.int32)


def block_scale(key, dims, shards, smallest, high):
    level = 1.0
    for dim, parts in shards:
        heights = jax.random.uniform(jax.random.fold_in(jax.random.fold_in(key, 6), dim), (parts,), jnp.float32, smallest / len(shards), high / len(shards))
        level = level * jnp.repeat(jnp.exp(heights), dims[dim] // parts).reshape((-1,) + (1,) * (len(dims) - 1 - dim))
    return level


def length_profile(number_of, total, reach, skew):
    portions = [(1 << 20) // math.isqrt(rank ** skew) + 1 for rank in range(2, number_of + 1)]
    rest, given = total - reach - (number_of - 1), [1] * (number_of - 1)
    while rest > 0:
        free = [i for i in range(number_of - 1) if given[i] < reach]
        whole, remaining = sum([portions[i] for i in free]), rest
        for i in free:
            more = min(reach - given[i], max(1, remaining * portions[i] // whole), rest)
            given[i] = given[i] + more
            rest = rest - more
    return np.array([reach] + given)


def ragged(key, amount, total, limit, slope):
    if amount == 2:
        one = jax.random.randint(key, (), max(1, total - limit), min(limit, total - 1) + 1)
        return jnp.stack([one, total - one])
    lengths = jnp.asarray(length_profile(amount, total, limit, slope), jnp.int32)
    pairs = (amount - 1) // 2
    source_of, receiver = lengths[1:1 + 2 * pairs:2], lengths[2:2 + 2 * pairs:2]
    room = jnp.minimum(source_of - 1, limit - receiver)
    moved = jax.random.randint(jax.random.fold_in(key, 1), (pairs,), 0, 1 << 20) % (room + 1)
    lengths = lengths.at[1:1 + 2 * pairs:2].set(source_of - moved).at[2:2 + 2 * pairs:2].set(receiver + moved)
    return lengths[jax.random.permutation(jax.random.fold_in(key, 2), amount)]


def centred(rng, shape, scale, most, shards=(), kind=jnp.bfloat16):
    drawn = scale * jax.random.normal(rng, shape, jnp.float32)
    if shards:
        drawn = drawn * block_scale(rng, shape, shards, -0.22, 0.18)
    return jnp.clip(drawn, -most, most).astype(kind)


def setup_inputs(seed: int = 0) -> dict:
    seeds = jax.random.split(jax.random.key(seed), 9)
    queries = draw_queries(jax.random.fold_in(seeds[8], 71), 0)
    new_keys = centred(seeds[1], (ROLLOUTS, NEW, KVH, HD), 1.0, 4.0, ((1, 128),))
    turn_value_rows = centred(seeds[2], (ROLLOUTS, NEW, KVH, HD), 1.0, 4.0, ((1, 128),))
    cache_keys = draw_cache_keys(jax.random.fold_in(seeds[8], 71), 0)
    cache_values = centred(seeds[4], (ROLLOUTS, CACHE, KVH, HD), 1.0, 4.0, ((1, 16), (2, 8)))
    cached_len = ragged(seeds[5], ROLLOUTS, CACHE * (ROLLOUTS + 1) // 2, CACHE, 1).astype(jnp.int32)
    new_len = draw_new_len(jax.random.fold_in(seeds[8], 71), 0)
    fold = jax.random.permutation(seeds[7], SHARDS).astype(jnp.int32)
    return dict(queries=queries, new_keys=new_keys, turn_value_rows=turn_value_rows, cache_keys=cache_keys, cache_values=cache_values, cached_len=cached_len, new_len=new_len, fold=fold)


NEG_FILL = -1e30


def reference(queries, new_keys, turn_value_rows, cache_keys, cache_values, cached_len, new_len, fold):
    score_scale = HD ** -0.5
    logical = (fold[:, None] * CACHE_DEV + jnp.arange(CACHE_DEV, dtype=jnp.int32)[None, :]).reshape(-1).astype(jnp.int32)
    positions = jnp.arange(NEW, dtype=jnp.int32)
    causal = positions[None, :] <= positions[:, None]
    output_list = []
    for rollout in range(ROLLOUTS):
        cache_open = logical < cached_len[rollout]
        allowed = jnp.concatenate([jnp.broadcast_to(cache_open[None, :], (NEW, CACHE)), causal], axis=1)
        key_stack = jnp.concatenate([cache_keys[rollout], new_keys[rollout]], axis=0)
        value_stack = jnp.concatenate([cache_values[rollout], turn_value_rows[rollout]], axis=0)
        grouped_q = queries[rollout].reshape(NEW, KVH, GROUP, HD).transpose(1, 2, 0, 3)

        def per_group(member):
            group_q, group_k, group_v = member

            def per_head(head_q):
                scores = jnp.dot(head_q, group_k.T, preferred_element_type=jnp.float32) * score_scale
                scores = jnp.where(allowed, scores, NEG_FILL)
                row_top = jnp.max(scores, axis=1)
                weights = jnp.exp(scores - row_top[:, None])
                row_sum_overall = jnp.sum(weights, axis=1)
                summed = jnp.dot(weights.astype(jnp.bfloat16), group_v, preferred_element_type=jnp.float32)
                return summed / row_sum_overall[:, None]

            return lax.map(per_head, group_q)

        attended = lax.map(per_group, (grouped_q, key_stack.transpose(1, 0, 2), value_stack.transpose(1, 0, 2)))
        attended = attended.transpose(2, 0, 1, 3).reshape(NEW, H, HD)
        live_rows = positions < new_len[rollout]
        output_list.append(jnp.where(live_rows[:, None, None], attended, 0.0).astype(jnp.bfloat16))
    return jnp.stack(output_list)
```

```python
import functools

import jax
import jax.numpy as jnp
from jax import lax
from jax.experimental import pallas as pl
from jax.experimental.pallas import tpu as pltpu
from jax.sharding import PartitionSpec as P

MESH = pl.DeviceIdType.MESH
BF16 = jnp.bfloat16
F32 = jnp.float32
LOG2E = 1.4426950408889634
CLOSED = -1e30
ROWS = 128
TAIL = 16
CHUNK = 512


def flipped(index, mask, bits):
    result = 0
    for k in range(bits):
        bit = lax.rem(lax.div(index, 1 << k), 2)
        result = result + ((1 - bit) if (mask >> k) & 1 else bit) * (1 << k)
    return result


def contract(a, b, ca, cb):
    return lax.dot_general(a, b, (((ca,), (cb,)), ((), ())), preferred_element_type=F32)


def await_bytes(ref, sem):
    pltpu.make_async_copy(ref, ref, sem).wait()


def kernel(
    q_hbm, nk_ref, nv_ref, k_hbm, v_hbm, clen_ref, nlen_ref, fold_ref, out_ref,
    qall, kbuf, vaug, s0, s1, m0, m1, oloc, r1, cp, r2, fin, onew, lnew, stage_f, stage, kva, asm,
    k_sem, v_sem, own_sem, a_send, a_recv, kv_send, kv_recv, b_send, b_recv,
    r1_send, r1_recv, r2_send, r2_recv, r3_send, r3_recv, r3_own,
):
    c = lax.axis_index("ctx")
    t = lax.axis_index("tp")
    rollouts = k_hbm.shape[0]
    span = k_hbm.shape[1]
    slots = qall.shape[1]
    tps = stage.shape[0]
    group = ROWS // tps
    scale = 128 ** -0.5 * LOG2E
    ctx_peer = [flipped(c, j, 4) for j in range(slots)]
    tp_peer = [flipped(t, i, 3) for i in range(tps)]
    partner = ctx_peer[1]
    my_rows = pl.ds(pl.multiple_of(t * group, group), group)

    def rows_of(i):
        return pl.ds(pl.multiple_of(tp_peer[i] * group, group), group)

    def remote(src, dst, send, recv, ctx, tp):
        pltpu.make_async_remote_copy(
            src_ref=src, dst_ref=dst, send_sem=send, recv_sem=recv,
            device_id=(ctx, tp), device_id_type=MESH,
        ).start()

    own_copy = pltpu.make_async_copy(q_hbm.at[:, my_rows, :], qall.at[:, 0, my_rows, :], own_sem)
    own_copy.start()
    k_copies, v_copies = [], []
    for b in range(rollouts):
        k_copies.append(pltpu.make_async_copy(k_hbm.at[b], kbuf.at[b], k_sem.at[b]))
        v_copies.append(pltpu.make_async_copy(v_hbm.at[b], vaug.at[b, :, pl.ds(0, 128)], v_sem.at[b]))
        k_copies[b].start()
        v_copies[b].start()

    barrier = pltpu.get_barrier_semaphore()
    for i in range(1, tps):
        pl.semaphore_signal(barrier, inc=1, device_id=(c, tp_peer[i]), device_id_type=MESH)
    greeted = [1] + list(range(2, slots, 2))
    for j in greeted:
        pl.semaphore_signal(barrier, inc=1, device_id=(ctx_peer[j], t), device_id_type=MESH)

    stage_f[...] = jnp.zeros_like(stage_f)
    for b in range(rollouts):
        keys_f = nk_ref[b].astype(F32)
        vals_f = nv_ref[b].astype(F32)
        for i in range(tps):
            stage_f[i, b : b + 1, :] = keys_f[i : i + 1, :]
            stage_f[i, rollouts + b : rollouts + b + 1, :] = vals_f[i : i + 1, :]
    stage[...] = stage_f[...].astype(BF16)
    kva[pl.ds(t, 1)] = stage[pl.ds(t, 1)]

    pl.semaphore_wait(barrier, tps - 1 + len(greeted))

    def send_a(b):
        for i in range(1, tps):
            remote(q_hbm.at[b, rows_of(i), :], qall.at[b, 0, my_rows, :],
                   a_send.at[b], a_recv.at[b], c, tp_peer[i])

    def wait_a(b):
        await_bytes(qall.at[b, 0, pl.ds(0, ROWS - group), :], a_recv.at[b])

    send_a(0)
    for i in range(1, tps):
        remote(stage.at[tp_peer[i]], kva.at[t], kv_send, kv_recv, c, tp_peer[i])
    for b in range(1, rollouts):
        send_a(b)

    def send_b(b):
        for j in greeted:
            remote(qall.at[b, 0], qall.at[b, j], b_send.at[b], b_recv.at[b, j], ctx_peer[j], t)

    def wait_b(b, j):
        await_bytes(qall.at[b, j], b_recv.at[b, j])

    def pass_on(b, q):
        for j in (4 * q, 4 * q + 2):
            if j:
                wait_b(b, j)
                remote(qall.at[b, j], qall.at[b, j + 1], b_send.at[b], b_recv.at[b, j + 1], partner, t)

    def wait_odd(b, q):
        for j in (4 * q + 1, 4 * q + 3):
            wait_b(b, j)

    def prepare(b):
        open_count = clen_ref[b] - fold_ref[c] * span
        for r in range(0, span, 256):
            row = lax.broadcasted_iota(jnp.int32, (256, 128), 0) + r
            is_open = row < open_count
            first = kbuf[b, 0:16, :].astype(F32)[0:1, :]
            kbuf[b, r : r + 256, :] = jnp.where(
                is_open, kbuf[b, r : r + 256, :].astype(F32), first).astype(BF16)
            vaug[b, r : r + 256, 0:128] = jnp.where(
                is_open, vaug[b, r : r + 256, 0:128].astype(F32), 0.0).astype(BF16)
            vaug[b, r : r + 256, 128:256] = jnp.where(is_open, 1.0, 0.0).astype(BF16)

    eye = (lax.broadcasted_iota(jnp.int32, (ROWS, ROWS), 0)
           == lax.broadcasted_iota(jnp.int32, (ROWS, ROWS), 1))

    def score_tile(b, q, s_ref, m_ref):
        queries = qall[b, 4 * q : 4 * q + 4, 0:ROWS, :].reshape(4 * ROWS, 128)
        top = None
        for k in range(0, span, CHUNK):
            s = contract(queries, kbuf[b, k : k + CHUNK, :], 1, 1)
            s_ref[:, k : k + CHUNK] = s
            for x in range(0, CHUNK, 128):
                part = s[:, x : x + 128]
                top = part if top is None else jnp.maximum(top, part)
        m_ref[...] = jnp.broadcast_to(jnp.max(top, axis=1, keepdims=True) * scale, m_ref.shape)

    def stat_rows(stat):
        high = stat.astype(BF16).astype(F32)
        middle = (stat - high).astype(BF16).astype(F32)
        low = stat - high - middle
        row = lax.broadcasted_iota(jnp.int32, (TAIL, 128), 0)
        return jnp.where(row == 0, high, jnp.where(row == 1, middle, jnp.where(row == 2, low, 0.0))).astype(BF16)

    def stat_of(rows):
        return jnp.sum(rows.astype(F32), axis=0, keepdims=True)

    def diagonal(weight):
        return jnp.where(eye, jnp.broadcast_to(weight, (ROWS, ROWS)), 0.0).astype(BF16)

    def to_row(replicated):
        return jnp.sum(jnp.where(eye, replicated, 0.0), axis=0, keepdims=True)

    def finish(total, weight, top):
        live = weight > 0.0
        safe = jnp.where(live, weight, 1.0)
        return (jnp.where(live, total / safe, 0.0), jnp.where(live, top + jnp.log2(safe), CLOSED))

    def weigh_tile(b, q, s_ref, m_ref):
        top = m_ref[...]
        total = None
        for k in range(0, span, CHUNK):
            parts = []
            for x in range(k, k + CHUNK, 128):
                parts.append(jnp.exp2(s_ref[:, x : x + 128] * scale - top).astype(BF16))
            d = contract(jnp.concatenate(parts, axis=1), vaug[b, k : k + CHUNK, :], 1, 0)
            total = d if total is None else total + d
        mean, level = finish(total[:, 0:128], total[:, 128:256], top)
        mean = mean.astype(BF16)
        for g in range(4):
            rows = slice(g * ROWS, (g + 1) * ROWS)
            oloc[b, q, g // 2, g % 2, 0:ROWS, :] = mean[rows]
            oloc[b, q, g // 2, g % 2, ROWS : ROWS + TAIL, :] = stat_rows(to_row(level[rows]))

    def blend(pieces, levels):
        top = functools.reduce(jnp.maximum, levels)
        weights = [jnp.exp2(level - top) for level in levels]
        total = functools.reduce(jnp.add, weights)
        share = 1.0 / total
        left = jnp.concatenate([diagonal(weight * share) for weight in weights], axis=1)
        mixed = contract(left, jnp.concatenate(pieces, axis=0), 1, 0)
        return mixed, top + jnp.log2(total)

    def chip_blend(b, q):
        for g in range(2):
            mixed, level = blend(
                [oloc[b, q, g, 0, 0:ROWS, :], r1[b, q, g, 0:ROWS, :]],
                [stat_of(oloc[b, q, g, 0, ROWS : ROWS + TAIL, :]), stat_of(r1[b, q, g, ROWS : ROWS + TAIL, :])],
            )
            cp[b, 2 * q + g, 0:ROWS, :] = mixed.astype(BF16)
            cp[b, 2 * q + g, ROWS : ROWS + TAIL, :] = stat_rows(level)

    def new_part(b):
        blocks = [qall[b, j, ROWS : ROWS + TAIL, :].astype(F32) for j in range(slots)]
        keys = jnp.concatenate([x[0:8] for x in blocks], axis=0).astype(BF16)
        values = jnp.concatenate([x[8:16] for x in blocks], axis=0).astype(BF16)
        column = lax.broadcasted_iota(jnp.int32, (ROWS, ROWS), 1)
        position = lax.rem(column, tps)
        for j in range(slots):
            position = position + jnp.where(lax.div(column, tps) == j, ctx_peer[j] * tps, 0)
        row = lax.broadcasted_iota(jnp.int32, (ROWS, ROWS), 0)
        allowed = position <= c * tps + lax.div(row, group)
        s = jnp.where(allowed, contract(qall[b, 0, 0:ROWS, :], keys, 1, 1) * scale, CLOSED)
        top = jnp.max(s, axis=1, keepdims=True)
        p = jnp.exp2(s - top)
        weight = jnp.sum(p, axis=1, keepdims=True)
        mean = contract(p.astype(BF16), values, 1, 0) / weight
        onew[b] = mean.astype(BF16)
        lnew[b] = jnp.broadcast_to(
            to_row(jnp.broadcast_to(top + jnp.log2(weight), (ROWS, ROWS))), (8, 128))

    def last_blend(b):
        pieces = [cp[b, 0, 0:ROWS, :]] + [r2[b, j, 0:ROWS, :] for j in range(1, slots // 2)] + [onew[b]]
        levels = [stat_of(cp[b, 0, ROWS : ROWS + TAIL, :])]
        levels += [stat_of(r2[b, j, ROWS : ROWS + TAIL, :]) for j in range(1, slots // 2)]
        levels += [lnew[b, 0:1, :]]
        mixed, _ = blend(pieces, levels)
        token = c * tps + lax.div(lax.broadcasted_iota(jnp.int32, (ROWS, 128), 0), group)
        fin[b] = jnp.where(token < nlen_ref[b], mixed, 0.0).astype(BF16)

    def send_r1(b, q):
        remote(oloc.at[b, q, :, 1], r1.at[b, q], r1_send.at[b], r1_recv.at[b, q], partner, t)

    def wait_r1(b, q):
        await_bytes(r1.at[b, q], r1_recv.at[b, q])

    def send_r2(b, q):
        for j in (2 * q, 2 * q + 1):
            if j:
                remote(cp.at[b, j], r2.at[b, j], r2_send.at[b], r2_recv.at[b], ctx_peer[2 * j], t)

    def wait_r2(b):
        await_bytes(r2.at[b, pl.ds(1, slots // 2 - 1)], r2_recv.at[b])

    def send_r3(b):
        for i in range(1, tps):
            remote(fin.at[b, rows_of(i), :], out_ref.at[b, my_rows, :], r3_send, r3_recv, c, tp_peer[i])

    own_copy.wait()
    await_bytes(kva.at[pl.ds(0, tps - 1)], kv_recv)
    for b in range(rollouts):
        for i in range(tps):
            asm[b, i : i + 1, :] = kva[i].astype(F32)[b : b + 1, :]
            asm[b, tps + i : tps + i + 1, :] = kva[i].astype(F32)[rollouts + b : rollouts + b + 1, :]
    for b in range(rollouts):
        qall[b, 0, ROWS : ROWS + TAIL, :] = asm[b].astype(BF16)
    wait_a(0)
    send_b(0)
    k_copies[0].wait()
    v_copies[0].wait()
    prepare(0)
    pass_on(0, 0)
    pass_on(0, 1)
    wait_odd(0, 0)
    score_tile(0, 0, s0, m0)
    for b in range(1, rollouts):
        k_copies[b].wait()
        v_copies[b].wait()

    tiles = slots // 4

    def rollout_step(b, carry):
        more = b < rollouts - 1
        nb = jnp.minimum(b + 1, rollouts - 1)
        for q in range(tiles):
            cur, nxt = ((s0, m0), (s1, m1)) if q % 2 == 0 else ((s1, m1), (s0, m0))
            if q == 0:
                @pl.when(more)
                def _():
                    wait_a(nb)
                    send_b(nb)

                @pl.when(b > 0)
                def _():
                    wait_r1(b - 1, tiles - 1)
                    chip_blend(b - 1, tiles - 1)
                    send_r2(b - 1, tiles - 1)
            else:
                wait_r1(b, q - 1)
            if q == 2:
                @pl.when(b > 0)
                def _():
                    wait_r2(b - 1)
                    last_blend(b - 1)
                    send_r3(b - 1)
            if q + 2 < tiles:
                pass_on(b, q + 2)
            else:
                @pl.when(more)
                def _():
                    pass_on(nb, q + 2 - tiles)
            if q + 1 < tiles:
                wait_odd(b, q + 1)
                score_tile(b, q + 1, *nxt)
            else:
                @pl.when(more)
                def _():
                    wait_odd(nb, 0)
                    prepare(nb)
                score_tile(nb, 0, *nxt)
            weigh_tile(b, q, *cur)
            if q:
                chip_blend(b, q - 1)
            if q == tiles - 1:
                new_part(b)
            send_r1(b, q)
            if q:
                send_r2(b, q - 1)
        return carry

    lax.fori_loop(0, rollouts, rollout_step, 0)

    last = rollouts - 1
    wait_r1(last, tiles - 1)
    chip_blend(last, tiles - 1)
    send_r2(last, tiles - 1)
    wait_r2(last)
    last_blend(last)
    send_r3(last)
    keep = pltpu.make_async_copy(fin.at[:, my_rows, :], out_ref.at[:, my_rows, :], r3_own)
    keep.start()

    for b in range(rollouts):
        await_bytes(qall.at[b, 0, pl.ds(0, ROWS - group), :], a_send.at[b])
        await_bytes(qall.at[b, pl.ds(0, slots - 1)], b_send.at[b])
        await_bytes(r1.at[b], r1_send.at[b])
        await_bytes(r2.at[b, pl.ds(1, slots // 2 - 1)], r2_send.at[b])
    await_bytes(kva.at[pl.ds(0, tps - 1)], kv_send)
    await_bytes(fin.at[:, pl.ds(0, ROWS - group), :], r3_send)
    await_bytes(fin.at[:, pl.ds(0, ROWS - group), :], r3_recv)
    keep.wait()


def shards(queries, new_keys, turn_value_rows, cache_keys, cache_values, cached_len, new_len, fold):
    rollouts, span = cache_keys.shape[0], cache_keys.shape[1]
    slots, tps = lax.axis_size("ctx"), lax.axis_size("tp")
    tiles = slots // 4
    any_space = pl.BlockSpec(memory_space=pl.ANY)
    vmem = pl.BlockSpec(memory_space=pltpu.VMEM)
    smem = pl.BlockSpec(memory_space=pltpu.SMEM)
    dma = pltpu.SemaphoreType.DMA
    block = (ROWS + TAIL, 128)
    out = pl.pallas_call(
        kernel,
        out_shape=jax.ShapeDtypeStruct((rollouts, 128, 128), BF16),
        in_specs=[any_space, vmem, vmem, any_space, any_space, smem, smem, smem],
        out_specs=any_space,
        scratch_shapes=[
            pltpu.VMEM((rollouts, slots) + block, BF16),
            pltpu.VMEM((rollouts, span, 128), BF16),
            pltpu.VMEM((rollouts, span, 256), BF16),
            pltpu.VMEM((4 * ROWS, span), F32),
            pltpu.VMEM((4 * ROWS, span), F32),
            pltpu.VMEM((4 * ROWS, 128), F32),
            pltpu.VMEM((4 * ROWS, 128), F32),
            pltpu.VMEM((rollouts, tiles, 2, 2) + block, BF16),
            pltpu.VMEM((rollouts, tiles, 2) + block, BF16),
            pltpu.VMEM((rollouts, slots // 2) + block, BF16),
            pltpu.VMEM((rollouts, slots // 2) + block, BF16),
            pltpu.VMEM((rollouts, ROWS, 128), BF16),
            pltpu.VMEM((rollouts, ROWS, 128), BF16),
            pltpu.VMEM((rollouts, 8, 128), F32),
            pltpu.VMEM((tps, TAIL, 128), F32),
            pltpu.VMEM((tps, TAIL, 128), BF16),
            pltpu.VMEM((tps, TAIL, 128), BF16),
            pltpu.VMEM((rollouts, TAIL, 128), F32),
            dma((rollouts,)), dma((rollouts,)), dma,
            dma((rollouts,)), dma((rollouts,)),
            dma, dma,
            dma((rollouts,)), dma((rollouts, slots)),
            dma((rollouts,)), dma((rollouts, tiles)),
            dma((rollouts,)), dma((rollouts,)),
            dma, dma, dma,
        ],
        compiler_params=pltpu.CompilerParams(
            collective_id=0, has_side_effects=True, vmem_limit_bytes=56 << 20),
        name="turn_attention",
    )(
        queries[:, 0], new_keys[:, 0], turn_value_rows[:, 0],
        cache_keys[:, :, 0], cache_values[:, :, 0], cached_len, new_len, fold,
    )
    return out[:, None]


def solution(mesh):
    in_specs = (
        P(None, ("ctx", "tp"), None, None),
        P(None, ("ctx", "tp"), None, None),
        P(None, ("ctx", "tp"), None, None),
        P(None, "ctx", "tp", None),
        P(None, "ctx", "tp", None),
        P(),
        P(),
        P(),
    )
    out_specs = P(None, ("ctx", "tp"), None, None)
    return jax.shard_map(shards, mesh=mesh, in_specs=in_specs, out_specs=out_specs, check_vma=False)
```

```python
import functools

import jax
import jax.numpy as jnp
from jax import lax
from jax.experimental import pallas as pl
from jax.experimental.pallas import tpu as pltpu
from jax.sharding import PartitionSpec as P

MESH = pl.DeviceIdType.MESH
BF16 = jnp.bfloat16
F32 = jnp.float32
LOG2E = 1.4426950408889634
CLOSED = -1e30
ROWS = 128
TAIL = 16
CHUNK = 512
TILES = ((0, 1), (3, 4), (2, 5), (6, 7))
GREETED = (2, 6, 8, 4, 10, 14, 12, 1)
ORDER = ((0, 0), (0, 1), (1, 0), (1, 1), (0, 2), (0, 3), (1, 2), (1, 3),
         (2, 3), (2, 2), (2, 1), (2, 0), (3, 3), (3, 2), (3, 1), (3, 0))


def flipped(index, mask, bits):
    result = 0
    for k in range(bits):
        bit = lax.rem(lax.div(index, 1 << k), 2)
        result = result + ((1 - bit) if (mask >> k) & 1 else bit) * (1 << k)
    return result


def contract(a, b, ca, cb):
    return lax.dot_general(a, b, (((ca,), (cb,)), ((), ())), preferred_element_type=F32)


def await_bytes(ref, sem):
    pltpu.make_async_copy(ref, ref, sem).wait()


def kernel(
    q_hbm, nk_hbm, nv_hbm, k_hbm, v_hbm, clen_hbm, nlen_hbm, fold_hbm, out_ref,
    qall, kbuf, vaug, s0, s1, m0, m1, oloc, r1, cp, r2, fin, onew, lnew,
    nk_ref, nv_ref, stage_f, stage, kva, asm, kvg, clen_ref, nlen_ref, fold_ref,
    k_sem, v_sem, own_sem, small_sem, a_send, a_recv, kv_send, kv_recv, b_send, b_recv, g_send, g_recv,
    r1_send, r1_recv, r2_send, r2_recv, r3_send, r3_recv, r3_own,
):
    c = lax.axis_index("ctx")
    t = lax.axis_index("tp")
    rollouts = k_hbm.shape[0]
    span = k_hbm.shape[1]
    slots = qall.shape[1]
    tps = stage.shape[0]
    group = ROWS // tps
    scale = 128 ** -0.5 * LOG2E
    ctx_peer = [flipped(c, j, 4) for j in range(slots)]
    tp_peer = [flipped(t, i, 3) for i in range(tps)]
    partner = ctx_peer[1]
    my_rows = pl.ds(pl.multiple_of(t * group, group), group)

    def rows_of(i):
        return pl.ds(pl.multiple_of(tp_peer[i] * group, group), group)

    def remote(src, dst, send, recv, ctx, tp):
        pltpu.make_async_remote_copy(
            src_ref=src, dst_ref=dst, send_sem=send, recv_sem=recv,
            device_id=(ctx, tp), device_id_type=MESH,
        ).start()

    barrier = pltpu.get_barrier_semaphore()
    for i in range(1, tps):
        pl.semaphore_signal(barrier, inc=1, device_id=(c, tp_peer[i]), device_id_type=MESH)
    for j in GREETED:
        pl.semaphore_signal(barrier, inc=1, device_id=(ctx_peer[j], t), device_id_type=MESH)

    small = [
        pltpu.make_async_copy(src, dst, small_sem.at[i])
        for i, (src, dst) in enumerate((
            (nk_hbm, nk_ref), (nv_hbm, nv_ref), (clen_hbm, clen_ref), (nlen_hbm, nlen_ref), (fold_hbm, fold_ref)))
    ]
    for copy in small:
        copy.start()
    own_copy = pltpu.make_async_copy(q_hbm.at[:, my_rows, :], qall.at[:, 0, my_rows, :], own_sem)
    own_copy.start()
    k_copies, v_copies = [], []
    for b in range(rollouts):
        k_copies.append(pltpu.make_async_copy(k_hbm.at[b], kbuf.at[b], k_sem.at[b]))
        v_copies.append(pltpu.make_async_copy(v_hbm.at[b], vaug.at[b, :, pl.ds(0, 128)], v_sem.at[b]))
        k_copies[b].start()
        v_copies[b].start()

    for copy in small:
        copy.wait()
    stage_f[...] = jnp.zeros_like(stage_f)
    for b in range(rollouts):
        keys_f = nk_ref[b].astype(F32)
        vals_f = nv_ref[b].astype(F32)
        for i in range(tps):
            stage_f[i, b : b + 1, :] = keys_f[i : i + 1, :]
            stage_f[i, rollouts + b : rollouts + b + 1, :] = vals_f[i : i + 1, :]
    stage[...] = stage_f[...].astype(BF16)
    kva[pl.ds(t, 1)] = stage[pl.ds(t, 1)]

    pl.semaphore_wait(barrier, tps - 1 + len(GREETED))

    def send_a(b):
        for i in range(1, tps):
            remote(q_hbm.at[b, rows_of(i), :], qall.at[b, 0, my_rows, :],
                   a_send.at[b], a_recv.at[b], c, tp_peer[i])

    def wait_a(b):
        await_bytes(qall.at[b, 0, pl.ds(0, ROWS - group), :], a_recv.at[b])

    for b in range(rollouts):
        send_a(b)
    for i in range(1, tps):
        remote(stage.at[tp_peer[i]], kva.at[t], kv_send, kv_recv, c, tp_peer[i])

    def send_b(b):
        for j in GREETED:
            remote(qall.at[b, 0], qall.at[b, j], b_send.at[b], b_recv.at[b, j], ctx_peer[j], t)

    def pass_on(b, q):
        for p in TILES[q]:
            if p:
                await_bytes(qall.at[b, 2 * p], b_recv.at[b, 2 * p])
                remote(qall.at[b, 2 * p], qall.at[b, 2 * p + 1], b_send.at[b], b_recv.at[b, 2 * p + 1], partner, t)

    def wait_odd(b, q):
        for p in TILES[q]:
            await_bytes(qall.at[b, 2 * p + 1], b_recv.at[b, 2 * p + 1])

    def kv_pass_on():
        for j in range(2, slots, 2):
            await_bytes(kvg.at[j], g_recv.at[j])
            remote(kvg.at[j], kvg.at[j + 1], g_send, g_recv.at[j + 1], partner, t)

    def prepare(b):
        open_count = clen_ref[b] - fold_ref[c] * span
        for r in range(0, span, 256):
            row = lax.broadcasted_iota(jnp.int32, (256, 128), 0) + r
            is_open = row < open_count
            first = kbuf[b, 0:16, :].astype(F32)[0:1, :]
            kbuf[b, r : r + 256, :] = jnp.where(
                is_open, kbuf[b, r : r + 256, :].astype(F32), first).astype(BF16)
            vaug[b, r : r + 256, 0:128] = jnp.where(
                is_open, vaug[b, r : r + 256, 0:128].astype(F32), 0.0).astype(BF16)
            vaug[b, r : r + 256, 128:256] = jnp.where(is_open, 1.0, 0.0).astype(BF16)

    eye = (lax.broadcasted_iota(jnp.int32, (ROWS, ROWS), 0)
           == lax.broadcasted_iota(jnp.int32, (ROWS, ROWS), 1))

    def tile_queries(b, q):
        return jnp.concatenate([qall[b, 2 * p : 2 * p + 2] for p in TILES[q]], axis=0)

    def score_tile(b, queries, s_ref, m_ref):
        queries = queries.reshape(4 * ROWS, 128)
        top = None
        for k in range(0, span, CHUNK):
            s = contract(queries, kbuf[b, k : k + CHUNK, :], 1, 1)
            s_ref[:, k : k + CHUNK] = s
            for x in range(0, CHUNK, 128):
                part = s[:, x : x + 128]
                top = part if top is None else jnp.maximum(top, part)
        m_ref[...] = jnp.broadcast_to(jnp.max(top, axis=1, keepdims=True) * scale, m_ref.shape)

    def stat_rows(stat):
        high = stat.astype(BF16).astype(F32)
        middle = (stat - high).astype(BF16).astype(F32)
        low = stat - high - middle
        row = lax.broadcasted_iota(jnp.int32, (TAIL, 128), 0)
        return jnp.where(row == 0, high, jnp.where(row == 1, middle, jnp.where(row == 2, low, 0.0))).astype(BF16)

    def stat_of(rows):
        return jnp.sum(rows.astype(F32), axis=0, keepdims=True)

    def diagonal(weight):
        return jnp.where(eye, jnp.broadcast_to(weight, (ROWS, ROWS)), 0.0).astype(BF16)

    def to_row(replicated):
        return jnp.sum(jnp.where(eye, replicated, 0.0), axis=0, keepdims=True)

    def finish(total, weight, top):
        live = weight > 0.0
        safe = jnp.where(live, weight, 1.0)
        return (jnp.where(live, total / safe, 0.0), jnp.where(live, top + jnp.log2(safe), CLOSED))

    def weigh_tile(b, q, s_ref, m_ref):
        top = m_ref[...]
        total = None
        for k in range(0, span, CHUNK):
            parts = []
            for x in range(k, k + CHUNK, 128):
                parts.append(jnp.exp2(s_ref[:, x : x + 128] * scale - top).astype(BF16))
            d = contract(jnp.concatenate(parts, axis=1), vaug[b, k : k + CHUNK, :], 1, 0)
            total = d if total is None else total + d
        mean, level = finish(total[:, 0:128], total[:, 128:256], top)
        mean = mean.astype(BF16)
        for g in range(4):
            rows = slice(g * ROWS, (g + 1) * ROWS)
            oloc[b, q, g // 2, g % 2, 0:ROWS, :] = mean[rows]
            oloc[b, q, g // 2, g % 2, ROWS : ROWS + TAIL, :] = stat_rows(to_row(level[rows]))

    def blend(pieces, levels):
        top = functools.reduce(jnp.maximum, levels)
        weights = [jnp.exp2(level - top) for level in levels]
        total = functools.reduce(jnp.add, weights)
        share = 1.0 / total
        left = jnp.concatenate([diagonal(weight * share) for weight in weights], axis=1)
        mixed = contract(left, jnp.concatenate(pieces, axis=0), 1, 0)
        return mixed, top + jnp.log2(total)

    def chip_blend(b, q):
        for g, pair in enumerate(TILES[q]):
            mixed, level = blend(
                [oloc[b, q, g, 0, 0:ROWS, :], r1[b, q, g, 0:ROWS, :]],
                [stat_of(oloc[b, q, g, 0, ROWS : ROWS + TAIL, :]), stat_of(r1[b, q, g, ROWS : ROWS + TAIL, :])],
            )
            cp[b, pair, 0:ROWS, :] = mixed.astype(BF16)
            cp[b, pair, ROWS : ROWS + TAIL, :] = stat_rows(level)

    def new_part(b):
        blocks = [kvg[j, b].astype(F32) for j in range(slots)]
        keys = jnp.concatenate([x[0:8] for x in blocks], axis=0).astype(BF16)
        values = jnp.concatenate([x[8:16] for x in blocks], axis=0).astype(BF16)
        column = lax.broadcasted_iota(jnp.int32, (ROWS, ROWS), 1)
        position = lax.rem(column, tps)
        for j in range(slots):
            position = position + jnp.where(lax.div(column, tps) == j, ctx_peer[j] * tps, 0)
        row = lax.broadcasted_iota(jnp.int32, (ROWS, ROWS), 0)
        allowed = position <= c * tps + lax.div(row, group)
        s = jnp.where(allowed, contract(qall[b, 0, 0:ROWS, :], keys, 1, 1) * scale, CLOSED)
        top = jnp.max(s, axis=1, keepdims=True)
        p = jnp.exp2(s - top)
        weight = jnp.sum(p, axis=1, keepdims=True)
        mean = contract(p.astype(BF16), values, 1, 0) / weight
        onew[b] = mean.astype(BF16)
        lnew[b] = jnp.broadcast_to(
            to_row(jnp.broadcast_to(top + jnp.log2(weight), (ROWS, ROWS))), (8, 128))

    def last_blend(b):
        sources = [cp.at[b, 0]] + [r2.at[b, p] for p in range(1, slots // 2)]
        pieces = [x[0:ROWS, :] for x in sources] + [onew[b]]
        levels = [stat_of(x[ROWS : ROWS + TAIL, :]) for x in sources] + [lnew[b, 0:1, :]]
        mixed, _ = blend(pieces, levels)
        token = c * tps + lax.div(lax.broadcasted_iota(jnp.int32, (ROWS, 128), 0), group)
        fin[b] = jnp.where(token < nlen_ref[b], mixed, 0.0).astype(BF16)

    def send_r1(b, q):
        remote(oloc.at[b, q, :, 1], r1.at[b, q], r1_send.at[b], r1_recv.at[b, q], partner, t)

    def wait_r1(b, q):
        await_bytes(r1.at[b, q], r1_recv.at[b, q])

    def send_r2(b, q):
        for p in TILES[q]:
            if p:
                remote(cp.at[b, p], r2.at[b, p], r2_send.at[b], r2_recv.at[b], ctx_peer[2 * p], t)

    def wait_r2(b):
        await_bytes(r2.at[b, pl.ds(1, slots // 2 - 1)], r2_recv.at[b])

    def send_r3(b):
        for i in range(1, tps):
            remote(fin.at[b, rows_of(i), :], out_ref.at[b, my_rows, :], r3_send, r3_recv, c, tp_peer[i])

    for b in range(rollouts):
        k_copies[b].wait()
        v_copies[b].wait()
        prepare(b)
    own_copy.wait()
    wait_a(0)
    send_b(0)
    wait_a(1)
    send_b(1)
    pass_on(0, 0)
    pass_on(0, 1)
    wait_odd(0, 0)
    bufs = ((s0, m0), (s1, m1))
    score_tile(0, tile_queries(0, 0), *bufs[0])

    def kv_start():
        await_bytes(kva.at[pl.ds(0, tps - 1)], kv_recv)
        for i in range(tps):
            block = kva[i].astype(F32)
            for b in range(rollouts):
                asm[b, i : i + 1, :] = block[b : b + 1, :]
                asm[b, tps + i : tps + i + 1, :] = block[rollouts + b : rollouts + b + 1, :]
        kvg[0] = asm[...].astype(BF16)
        for j in GREETED:
            remote(kvg.at[0], kvg.at[j], g_send, g_recv.at[j], ctx_peer[j], t)

    def kv_end():
        for j in range(1, slots, 2):
            await_bytes(kvg.at[j], g_recv.at[j])

    def begin(b):
        wait_a(b)
        send_b(b)

    def finish_rollout(b):
        last_blend(b)
        send_r3(b)

    count = len(ORDER)
    before, beside, after = ({n: [] for n in range(count + 2)} for _ in range(3))

    def at(when, step, what, *args):
        when[step].append((what, args))

    at(before, 0, begin, 2)
    at(before, 1, kv_start)
    at(before, 3, begin, 3)
    at(before, 7, kv_pass_on)
    at(before, 9, kv_end)
    for n, (b, q) in enumerate(ORDER):
        if n >= 2:
            at(before, n - 2, pass_on, b, q)
    for n, (b, q) in enumerate(ORDER):
        if n >= 1:
            at(before, n - 1, wait_odd, b, q)
        at(after, n, send_r1, b, q)
        at(before, n + 2, wait_r1, b, q)
        at(beside, n + 2, chip_blend, b, q)
        at(after, n + 2, send_r2, b, q)
    for b in range(rollouts):
        at(beside, 9 + b, new_part, b)
    for b, step in ((0, 12), (1, 14)):
        at(before, step, wait_r2, b)
        at(beside, step, last_blend, b)
        at(after, step, send_r3, b)

    for n, (b, q) in enumerate(ORDER):
        for what, args in before[n]:
            what(*args)
        if n + 1 < len(ORDER):
            nb, nq = ORDER[n + 1]
            score_tile(nb, tile_queries(nb, nq), *bufs[(n + 1) % 2])
        weigh_tile(b, q, *bufs[n % 2])
        for what, args in beside[n] + after[n]:
            what(*args)
    for end in (count, count + 1):
        for what, args in before[end] + beside[end] + after[end]:
            what(*args)
    for b in (2, 3):
        wait_r2(b)
        finish_rollout(b)
    keep = pltpu.make_async_copy(fin.at[:, my_rows, :], out_ref.at[:, my_rows, :], r3_own)
    keep.start()

    for b in range(rollouts):
        await_bytes(qall.at[b, 0, pl.ds(0, ROWS - group), :], a_send.at[b])
        await_bytes(qall.at[b, pl.ds(0, slots - 1)], b_send.at[b])
        await_bytes(r1.at[b], r1_send.at[b])
        await_bytes(r2.at[b, pl.ds(1, slots // 2 - 1)], r2_send.at[b])
    await_bytes(kva.at[pl.ds(0, tps - 1)], kv_send)
    await_bytes(kvg.at[pl.ds(0, slots - 1)], g_send)
    await_bytes(fin.at[:, pl.ds(0, ROWS - group), :], r3_send)
    await_bytes(fin.at[:, pl.ds(0, ROWS - group), :], r3_recv)
    keep.wait()


def shards(queries, new_keys, turn_value_rows, cache_keys, cache_values, cached_len, new_len, fold):
    rollouts, span = cache_keys.shape[0], cache_keys.shape[1]
    slots, tps = lax.axis_size("ctx"), lax.axis_size("tp")
    tiles = slots // 4
    any_space = pl.BlockSpec(memory_space=pl.ANY)
    dma = pltpu.SemaphoreType.DMA
    block = (ROWS + TAIL, 128)
    out = pl.pallas_call(
        kernel,
        out_shape=jax.ShapeDtypeStruct((rollouts, 128, 128), BF16),
        in_specs=[any_space] * 8,
        out_specs=any_space,
        scratch_shapes=[
            pltpu.VMEM((rollouts, slots, ROWS, 128), BF16),
            pltpu.VMEM((rollouts, span, 128), BF16),
            pltpu.VMEM((rollouts, span, 256), BF16),
            pltpu.VMEM((4 * ROWS, span), F32),
            pltpu.VMEM((4 * ROWS, span), F32),
            pltpu.VMEM((4 * ROWS, 128), F32),
            pltpu.VMEM((4 * ROWS, 128), F32),
            pltpu.VMEM((rollouts, tiles, 2, 2) + block, BF16),
            pltpu.VMEM((rollouts, tiles, 2) + block, BF16),
            pltpu.VMEM((rollouts, slots // 2) + block, BF16),
            pltpu.VMEM((rollouts, slots // 2) + block, BF16),
            pltpu.VMEM((rollouts, ROWS, 128), BF16),
            pltpu.VMEM((rollouts, ROWS, 128), BF16),
            pltpu.VMEM((rollouts, 8, 128), F32),
            pltpu.VMEM((rollouts, tps, 128), BF16),
            pltpu.VMEM((rollouts, tps, 128), BF16),
            pltpu.VMEM((tps, TAIL, 128), F32),
            pltpu.VMEM((tps, TAIL, 128), BF16),
            pltpu.VMEM((tps, TAIL, 128), BF16),
            pltpu.VMEM((rollouts, TAIL, 128), F32),
            pltpu.VMEM((slots, rollouts, TAIL, 128), BF16),
            pltpu.SMEM((rollouts,), jnp.int32), pltpu.SMEM((rollouts,), jnp.int32),
            pltpu.SMEM((slots,), jnp.int32),
            dma((rollouts,)), dma((rollouts,)), dma, dma((5,)),
            dma((rollouts,)), dma((rollouts,)),
            dma, dma,
            dma((rollouts,)), dma((rollouts, slots)),
            dma, dma((slots,)),
            dma((rollouts,)), dma((rollouts, tiles)),
            dma((rollouts,)), dma((rollouts,)),
            dma, dma, dma,
        ],
        compiler_params=pltpu.CompilerParams(
            collective_id=0, has_side_effects=True, vmem_limit_bytes=56 << 20),
        name="turn_attention",
    )(
        queries[:, 0], new_keys[:, 0], turn_value_rows[:, 0],
        cache_keys[:, :, 0], cache_values[:, :, 0], cached_len, new_len, fold,
    )
    return out[:, None]


def solution(mesh):
    in_specs = (
        P(None, ("ctx", "tp"), None, None),
        P(None, ("ctx", "tp"), None, None),
        P(None, ("ctx", "tp"), None, None),
        P(None, "ctx", "tp", None),
        P(None, "ctx", "tp", None),
        P(),
        P(),
        P(),
    )
    out_specs = P(None, ("ctx", "tp"), None, None)
    return jax.shard_map(shards, mesh=mesh, in_specs=in_specs, out_specs=out_specs, check_vma=False)
```

```python
import functools

import jax
import jax.numpy as jnp
from jax import lax
from jax.experimental import pallas as pl
from jax.experimental.pallas import tpu as pltpu
from jax.sharding import PartitionSpec as P

MESH = pl.DeviceIdType.MESH
BF16 = jnp.bfloat16
F32 = jnp.float32
LOG2E = 1.4426950408889634
CLOSED = -1e30
ROWS = 128
TAIL = 16
CHUNK = 512
NEAR = (2, 6, 8, 4)
FAR = (10, 14, 12)
LAST = (3, 1)
GREETED = NEAR + FAR + (1,) + tuple(2 * p + 1 for p in LAST)
ORDER = (
    ((0, 0), (1, 0)), ((2, 0), (3, 0)),
    ((0, 1), (0, 3)), ((0, 4), (0, 2)), ((0, 5), (0, 6)), ((0, 7), (1, 1)),
    ((1, 3), (1, 4)), ((1, 2), (1, 5)), ((1, 6), (1, 7)),
    ((2, 7), (2, 6)), ((2, 5), (2, 2)), ((2, 4), (2, 3)), ((2, 1), (3, 7)),
    ((3, 6), (3, 5)), ((3, 2), (3, 4)), ((3, 3), (3, 1)),
)


def flipped(index, mask, bits):
    result = 0
    for k in range(bits):
        bit = lax.rem(lax.div(index, 1 << k), 2)
        result = result + ((1 - bit) if (mask >> k) & 1 else bit) * (1 << k)
    return result


def contract(a, b, ca, cb):
    return lax.dot_general(a, b, (((ca,), (cb,)), ((), ())), preferred_element_type=F32)


def await_bytes(ref, sem):
    pltpu.make_async_copy(ref, ref, sem).wait()


def kernel(
    q_hbm, nk_hbm, nv_hbm, k_hbm, v_hbm, clen_hbm, nlen_hbm, fold_hbm, out_ref,
    qall, kbuf, vaug, s0, s1, m0, m1, oloc, r1, cp, r2, rx, fin, onew, lnew,
    nk_ref, nv_ref, stage_f, stage, kva, asm, kvg, clen_ref, nlen_ref, fold_ref,
    k_sem, v_sem, own_sem, small_sem, a_send, a_recv, kv_send, kv_recv, b_send, b_recv, g_send, g_recv,
    r1_send, r1_recv, r2_send, r2_recv, rx_send, rx_recv, r3_send, r3_recv, r3_own,
):
    c = lax.axis_index("ctx")
    t = lax.axis_index("tp")
    rollouts = k_hbm.shape[0]
    span = k_hbm.shape[1]
    slots = qall.shape[1]
    tps = stage.shape[0]
    group = ROWS // tps
    scale = 128 ** -0.5 * LOG2E
    ctx_peer = [flipped(c, j, 4) for j in range(slots)]
    tp_peer = [flipped(t, i, 3) for i in range(tps)]
    partner = ctx_peer[1]
    my_rows = pl.ds(pl.multiple_of(t * group, group), group)

    def rows_of(i):
        return pl.ds(pl.multiple_of(tp_peer[i] * group, group), group)

    def remote(src, dst, send, recv, ctx, tp):
        pltpu.make_async_remote_copy(
            src_ref=src, dst_ref=dst, send_sem=send, recv_sem=recv,
            device_id=(ctx, tp), device_id_type=MESH,
        ).start()

    barrier = pltpu.get_barrier_semaphore()
    for i in range(1, tps):
        pl.semaphore_signal(barrier, inc=1, device_id=(c, tp_peer[i]), device_id_type=MESH)
    for j in GREETED:
        pl.semaphore_signal(barrier, inc=1, device_id=(ctx_peer[j], t), device_id_type=MESH)

    small = [
        pltpu.make_async_copy(src, dst, small_sem.at[i])
        for i, (src, dst) in enumerate((
            (nk_hbm, nk_ref), (nv_hbm, nv_ref), (clen_hbm, clen_ref), (nlen_hbm, nlen_ref), (fold_hbm, fold_ref)))
    ]
    for copy in small:
        copy.start()
    own_copy = pltpu.make_async_copy(q_hbm.at[:, my_rows, :], qall.at[:, 0, my_rows, :], own_sem)
    own_copy.start()
    k_copies, v_copies = [], []
    for b in range(rollouts):
        k_copies.append(pltpu.make_async_copy(k_hbm.at[b], kbuf.at[b], k_sem.at[b]))
        v_copies.append(pltpu.make_async_copy(v_hbm.at[b], vaug.at[b, :, pl.ds(0, 128)], v_sem.at[b]))
        k_copies[b].start()
        v_copies[b].start()

    for copy in small:
        copy.wait()
    stage_f[...] = jnp.zeros_like(stage_f)
    for b in range(rollouts):
        keys_f = nk_ref[b].astype(F32)
        vals_f = nv_ref[b].astype(F32)
        for i in range(tps):
            stage_f[i, b : b + 1, :] = keys_f[i : i + 1, :]
            stage_f[i, rollouts + b : rollouts + b + 1, :] = vals_f[i : i + 1, :]
    stage[...] = stage_f[...].astype(BF16)
    kva[pl.ds(t, 1)] = stage[pl.ds(t, 1)]

    pl.semaphore_wait(barrier, tps - 1 + len(GREETED))

    def send_a(b):
        for i in range(1, tps):
            remote(q_hbm.at[b, rows_of(i), :], qall.at[b, 0, my_rows, :],
                   a_send.at[b], a_recv.at[b], c, tp_peer[i])

    def wait_a(b):
        await_bytes(qall.at[b, 0, pl.ds(0, ROWS - group), :], a_recv.at[b])

    for b in range(rollouts):
        send_a(b)
    for i in range(1, tps):
        remote(stage.at[tp_peer[i]], kva.at[t], kv_send, kv_recv, c, tp_peer[i])

    def send_b(b, *to):
        for j in to:
            remote(qall.at[b, 0], qall.at[b, j], b_send.at[b], b_recv.at[b, j], ctx_peer[j], t)

    def pass_on(*pairs):
        for b, p in pairs:
            await_bytes(qall.at[b, 2 * p], b_recv.at[b, 2 * p])
            remote(qall.at[b, 2 * p], qall.at[b, 2 * p + 1], b_send.at[b], b_recv.at[b, 2 * p + 1], partner, t)

    def wait_odd(*pairs):
        for b, p in pairs:
            await_bytes(qall.at[b, 2 * p + 1], b_recv.at[b, 2 * p + 1])

    def kv_pass_on():
        for j in range(2, slots, 2):
            await_bytes(kvg.at[j], g_recv.at[j])
            remote(kvg.at[j], kvg.at[j + 1], g_send, g_recv.at[j + 1], partner, t)

    def prepare(b):
        open_count = clen_ref[b] - fold_ref[c] * span
        for r in range(0, span, 256):
            row = lax.broadcasted_iota(jnp.int32, (256, 128), 0) + r
            is_open = row < open_count
            first = kbuf[b, 0:16, :].astype(F32)[0:1, :]
            kbuf[b, r : r + 256, :] = jnp.where(
                is_open, kbuf[b, r : r + 256, :].astype(F32), first).astype(BF16)
            vaug[b, r : r + 256, 0:128] = jnp.where(
                is_open, vaug[b, r : r + 256, 0:128].astype(F32), 0.0).astype(BF16)
            vaug[b, r : r + 256, 128:256] = jnp.where(is_open, 1.0, 0.0).astype(BF16)

    eye = (lax.broadcasted_iota(jnp.int32, (ROWS, ROWS), 0)
           == lax.broadcasted_iota(jnp.int32, (ROWS, ROWS), 1))

    def by_rollout(pairs):
        if pairs[0][0] == pairs[1][0]:
            return [(pairs[0][0], [p for _, p in pairs], slice(0, 4 * ROWS))]
        return [(b, [p], slice(2 * ROWS * i, 2 * ROWS * (i + 1))) for i, (b, p) in enumerate(pairs)]

    def score_step(pairs, s_ref, m_ref):
        for b, members, rows in by_rollout(pairs):
            queries = jnp.concatenate([qall[b, 2 * p : 2 * p + 2] for p in members], axis=0)
            queries = queries.reshape(2 * ROWS * len(members), 128)
            top = None
            for k in range(0, span, CHUNK):
                s = contract(queries, kbuf[b, k : k + CHUNK, :], 1, 1)
                s_ref[rows, k : k + CHUNK] = s
                for x in range(0, CHUNK, 128):
                    part = s[:, x : x + 128]
                    top = part if top is None else jnp.maximum(top, part)
            m_ref[rows, :] = jnp.broadcast_to(jnp.max(top, axis=1, keepdims=True) * scale, top.shape)

    def stat_rows(stat):
        high = stat.astype(BF16).astype(F32)
        middle = (stat - high).astype(BF16).astype(F32)
        low = stat - high - middle
        row = lax.broadcasted_iota(jnp.int32, (TAIL, 128), 0)
        return jnp.where(row == 0, high, jnp.where(row == 1, middle, jnp.where(row == 2, low, 0.0))).astype(BF16)

    def stat_of(rows):
        return jnp.sum(rows.astype(F32), axis=0, keepdims=True)

    def diagonal(weight):
        return jnp.where(eye, jnp.broadcast_to(weight, (ROWS, ROWS)), 0.0).astype(BF16)

    def to_row(replicated):
        return jnp.sum(jnp.where(eye, replicated, 0.0), axis=0, keepdims=True)

    def finish(total, weight, top):
        live = weight > 0.0
        safe = jnp.where(live, weight, 1.0)
        return (jnp.where(live, total / safe, 0.0), jnp.where(live, top + jnp.log2(safe), CLOSED))

    def weigh_step(pairs, s_ref, m_ref):
        for b, members, rows in by_rollout(pairs):
            top = m_ref[rows, :]
            total = None
            for k in range(0, span, CHUNK):
                parts = []
                for x in range(k, k + CHUNK, 128):
                    parts.append(jnp.exp2(s_ref[rows, x : x + 128] * scale - top).astype(BF16))
                d = contract(jnp.concatenate(parts, axis=1), vaug[b, k : k + CHUNK, :], 1, 0)
                total = d if total is None else total + d
            mean, level = finish(total[:, 0:128], total[:, 128:256], top)
            mean = mean.astype(BF16)
            for i, p in enumerate(members):
                for core in range(2):
                    at_rows = slice((2 * i + core) * ROWS, (2 * i + core + 1) * ROWS)
                    oloc[b, p, core, 0:ROWS, :] = mean[at_rows]
                    oloc[b, p, core, ROWS : ROWS + TAIL, :] = stat_rows(to_row(level[at_rows]))

    def blend(pieces, levels):
        top = functools.reduce(jnp.maximum, levels)
        weights = [jnp.exp2(level - top) for level in levels]
        total = functools.reduce(jnp.add, weights)
        share = 1.0 / total
        left = jnp.concatenate([diagonal(weight * share) for weight in weights], axis=1)
        mixed = contract(left, jnp.concatenate(pieces, axis=0), 1, 0)
        return mixed, top + jnp.log2(total)

    def chip_blend(b, p):
        mixed, level = blend(
            [oloc[b, p, 0, 0:ROWS, :], r1[b, p, 0:ROWS, :]],
            [stat_of(oloc[b, p, 0, ROWS : ROWS + TAIL, :]), stat_of(r1[b, p, ROWS : ROWS + TAIL, :])],
        )
        cp[b, p, 0:ROWS, :] = mixed.astype(BF16)
        cp[b, p, ROWS : ROWS + TAIL, :] = stat_rows(level)

    def new_part(b):
        blocks = [kvg[j, b].astype(F32) for j in range(slots)]
        keys = jnp.concatenate([x[0:8] for x in blocks], axis=0).astype(BF16)
        values = jnp.concatenate([x[8:16] for x in blocks], axis=0).astype(BF16)
        column = lax.broadcasted_iota(jnp.int32, (ROWS, ROWS), 1)
        position = lax.rem(column, tps)
        for j in range(slots):
            position = position + jnp.where(lax.div(column, tps) == j, ctx_peer[j] * tps, 0)
        row = lax.broadcasted_iota(jnp.int32, (ROWS, ROWS), 0)
        allowed = position <= c * tps + lax.div(row, group)
        s = jnp.where(allowed, contract(qall[b, 0, 0:ROWS, :], keys, 1, 1) * scale, CLOSED)
        top = jnp.max(s, axis=1, keepdims=True)
        p = jnp.exp2(s - top)
        weight = jnp.sum(p, axis=1, keepdims=True)
        mean = contract(p.astype(BF16), values, 1, 0) / weight
        onew[b] = mean.astype(BF16)
        lnew[b] = jnp.broadcast_to(
            to_row(jnp.broadcast_to(top + jnp.log2(weight), (ROWS, ROWS))), (8, 128))

    def last_blend(b):
        sources = [cp.at[b, 0]] + [r2.at[b, p] for p in range(1, slots // 2)]
        if b == rollouts - 1:
            sources += [rx.at[i] for i in range(len(LAST))]
        pieces = [x[0:ROWS, :] for x in sources] + [onew[b]]
        levels = [stat_of(x[ROWS : ROWS + TAIL, :]) for x in sources] + [lnew[b, 0:1, :]]
        mixed, _ = blend(pieces, levels)
        token = c * tps + lax.div(lax.broadcasted_iota(jnp.int32, (ROWS, 128), 0), group)
        fin[b] = jnp.where(token < nlen_ref[b], mixed, 0.0).astype(BF16)

    def send_r1(b, p):
        remote(oloc.at[b, p, 1], r1.at[b, p], r1_send.at[b], r1_recv.at[b, p], partner, t)

    def wait_r1(b, p):
        await_bytes(r1.at[b, p], r1_recv.at[b, p])

    def send_r2(b, p):
        if p:
            remote(cp.at[b, p], r2.at[b, p], r2_send.at[b], r2_recv.at[b], ctx_peer[2 * p], t)

    def send_last(b):
        for i, p in enumerate(LAST):
            remote(oloc.at[b, p, 0], r2.at[b, p], r2_send.at[b], r2_recv.at[b], ctx_peer[2 * p], t)
            remote(oloc.at[b, p, 1], rx.at[i], rx_send, rx_recv, ctx_peer[2 * p + 1], t)

    def wait_r2(b):
        await_bytes(r2.at[b, pl.ds(1, slots // 2 - 1)], r2_recv.at[b])

    def send_r3(b):
        for i in range(1, tps):
            remote(fin.at[b, rows_of(i), :], out_ref.at[b, my_rows, :], r3_send, r3_recv, c, tp_peer[i])

    for b in range(rollouts):
        k_copies[b].wait()
        v_copies[b].wait()
        prepare(b)
    own_copy.wait()
    for b in range(rollouts):
        wait_a(b)
        send_b(b, 1)
    send_b(0, *NEAR)
    bufs = ((s0, m0), (s1, m1))
    wait_odd(*ORDER[0])
    score_step(ORDER[0], *bufs[0])

    def kv_start():
        await_bytes(kva.at[pl.ds(0, tps - 1)], kv_recv)
        for i in range(tps):
            block = kva[i].astype(F32)
            for b in range(rollouts):
                asm[b, i : i + 1, :] = block[b : b + 1, :]
                asm[b, tps + i : tps + i + 1, :] = block[rollouts + b : rollouts + b + 1, :]
        kvg[0] = asm[...].astype(BF16)
        for j in NEAR + FAR + (1,):
            remote(kvg.at[0], kvg.at[j], g_send, g_recv.at[j], ctx_peer[j], t)

    def kv_end():
        for j in range(1, slots, 2):
            await_bytes(kvg.at[j], g_recv.at[j])

    def finish_rollout(b):
        last_blend(b)
        send_r3(b)

    count = len(ORDER)
    before, beside, after = ({n: [] for n in range(count + 2)} for _ in range(3))

    def at(when, step, what, *args):
        when[step].append((what, args))

    at(before, 0, send_b, 0, *FAR)
    at(before, 1, pass_on, (0, 1), (0, 3), (0, 4))
    at(before, 1, send_b, 1, *NEAR, *FAR)
    at(before, 2, pass_on, (0, 2))
    at(before, 3, pass_on, (0, 5), (0, 6), (0, 7), (1, 1))
    at(before, 4, pass_on, (1, 3), (1, 4))
    at(before, 5, pass_on, (1, 2), (1, 5))
    at(before, 6, pass_on, (1, 6), (1, 7))
    for n in range(7, count - 2):
        at(before, n, pass_on, *ORDER[n + 2])
    for n in range(count - 1):
        at(before, n, wait_odd, *ORDER[n + 1])
    at(before, 2, kv_start)
    at(before, 3, send_b, 2, *NEAR, *FAR)
    at(before, 6, send_b, 3, *NEAR, *FAR)
    at(before, 8, kv_pass_on)
    at(before, 10, kv_end)
    for n, pairs in enumerate(ORDER[:-1]):
        for pair in pairs:
            at(after, n, send_r1, *pair)
    for n, pairs in enumerate(ORDER[:-1]):
        later = min(n + 2, count)
        for pair in pairs:
            at(before, later, wait_r1, *pair)
            at(beside, later, chip_blend, *pair)
            at(after, later, send_r2, *pair)
    at(after, count - 1, send_last, rollouts - 1)
    for b in range(rollouts):
        at(beside, 10 + b, new_part, b)
    for b, step in ((0, 12), (1, 14)):
        at(before, step, wait_r2, b)
        at(beside, step, last_blend, b)
        at(after, step, send_r3, b)

    for n, pairs in enumerate(ORDER):
        for what, args in before[n]:
            what(*args)
        if n + 1 < count:
            score_step(ORDER[n + 1], *bufs[(n + 1) % 2])
        weigh_step(pairs, *bufs[n % 2])
        for what, args in beside[n] + after[n]:
            what(*args)
    for what, args in before[count] + beside[count] + after[count]:
        what(*args)
    wait_r2(2)
    finish_rollout(2)
    wait_r2(3)
    await_bytes(rx, rx_recv)
    finish_rollout(3)
    keep = pltpu.make_async_copy(fin.at[:, my_rows, :], out_ref.at[:, my_rows, :], r3_own)
    keep.start()

    for b in range(rollouts):
        await_bytes(qall.at[b, 0, pl.ds(0, ROWS - group), :], a_send.at[b])
        await_bytes(qall.at[b, pl.ds(0, slots - 1)], b_send.at[b])
        await_bytes(r1.at[b, pl.ds(0, slots // 2 - (len(LAST) if b == rollouts - 1 else 0))], r1_send.at[b])
        await_bytes(r2.at[b, pl.ds(1, slots // 2 - 1)], r2_send.at[b])
    await_bytes(kva.at[pl.ds(0, tps - 1)], kv_send)
    await_bytes(rx, rx_send)
    await_bytes(kvg.at[pl.ds(0, slots - 1)], g_send)
    await_bytes(fin.at[:, pl.ds(0, ROWS - group), :], r3_send)
    await_bytes(fin.at[:, pl.ds(0, ROWS - group), :], r3_recv)
    keep.wait()


def shards(queries, new_keys, turn_value_rows, cache_keys, cache_values, cached_len, new_len, fold):
    rollouts, span = cache_keys.shape[0], cache_keys.shape[1]
    slots, tps = lax.axis_size("ctx"), lax.axis_size("tp")
    any_space = pl.BlockSpec(memory_space=pl.ANY)
    dma = pltpu.SemaphoreType.DMA
    block = (ROWS + TAIL, 128)
    out = pl.pallas_call(
        kernel,
        out_shape=jax.ShapeDtypeStruct((rollouts, 128, 128), BF16),
        in_specs=[any_space] * 8,
        out_specs=any_space,
        scratch_shapes=[
            pltpu.VMEM((rollouts, slots, ROWS, 128), BF16),
            pltpu.VMEM((rollouts, span, 128), BF16),
            pltpu.VMEM((rollouts, span, 256), BF16),
            pltpu.VMEM((4 * ROWS, span), F32),
            pltpu.VMEM((4 * ROWS, span), F32),
            pltpu.VMEM((4 * ROWS, 128), F32),
            pltpu.VMEM((4 * ROWS, 128), F32),
            pltpu.VMEM((rollouts, slots // 2, 2) + block, BF16),
            pltpu.VMEM((rollouts, slots // 2) + block, BF16),
            pltpu.VMEM((rollouts, slots // 2) + block, BF16),
            pltpu.VMEM((rollouts, slots // 2) + block, BF16),
            pltpu.VMEM((len(LAST),) + block, BF16),
            pltpu.VMEM((rollouts, ROWS, 128), BF16),
            pltpu.VMEM((rollouts, ROWS, 128), BF16),
            pltpu.VMEM((rollouts, 8, 128), F32),
            pltpu.VMEM((rollouts, tps, 128), BF16),
            pltpu.VMEM((rollouts, tps, 128), BF16),
            pltpu.VMEM((tps, TAIL, 128), F32),
            pltpu.VMEM((tps, TAIL, 128), BF16),
            pltpu.VMEM((tps, TAIL, 128), BF16),
            pltpu.VMEM((rollouts, TAIL, 128), F32),
            pltpu.VMEM((slots, rollouts, TAIL, 128), BF16),
            pltpu.SMEM((rollouts,), jnp.int32), pltpu.SMEM((rollouts,), jnp.int32),
            pltpu.SMEM((slots,), jnp.int32),
            dma((rollouts,)), dma((rollouts,)), dma, dma((5,)),
            dma((rollouts,)), dma((rollouts,)),
            dma, dma,
            dma((rollouts,)), dma((rollouts, slots)),
            dma, dma((slots,)),
            dma((rollouts,)), dma((rollouts, slots // 2)),
            dma((rollouts,)), dma((rollouts,)),
            dma, dma,
            dma, dma, dma,
        ],
        compiler_params=pltpu.CompilerParams(
            collective_id=0, has_side_effects=True, vmem_limit_bytes=56 << 20),
        name="turn_attention",
    )(
        queries[:, 0], new_keys[:, 0], turn_value_rows[:, 0],
        cache_keys[:, :, 0], cache_values[:, :, 0], cached_len, new_len, fold,
    )
    return out[:, None]


def solution(mesh):
    in_specs = (
        P(None, ("ctx", "tp"), None, None),
        P(None, ("ctx", "tp"), None, None),
        P(None, ("ctx", "tp"), None, None),
        P(None, "ctx", "tp", None),
        P(None, "ctx", "tp", None),
        P(),
        P(),
        P(),
    )
    out_specs = P(None, ("ctx", "tp"), None, None)
    return jax.shard_map(shards, mesh=mesh, in_specs=in_specs, out_specs=out_specs, check_vma=False)
```

```python
import functools

import jax
import jax.numpy as jnp
from jax import lax
from jax.experimental import pallas as pl
from jax.experimental.pallas import tpu as pltpu
from jax.sharding import PartitionSpec as P

MESH = pl.DeviceIdType.MESH
BF16 = jnp.bfloat16
F32 = jnp.float32
LOG2E = 1.4426950408889634
CLOSED = -1e30
ROWS = 128
TAIL = 16
CHUNK = 512
NEAR = (2, 6, 8, 4)
FAR = (10, 14, 12)
LAST = (3, 1, 6, 5)
GREETED = NEAR + FAR + (1,) + tuple(2 * p + 1 for p in LAST)
ORDER = (
    ((0, 0), (1, 0)), ((2, 0), (3, 0)),
    ((0, 1), (0, 3)), ((0, 4), (0, 2)), ((0, 5), (0, 6)), ((0, 7), (1, 1)),
    ((1, 3), (1, 4)), ((1, 2), (1, 5)), ((1, 6), (1, 7)),
    ((2, 7), (2, 6)), ((2, 5), (2, 2)), ((2, 4), (2, 3)), ((2, 1), (3, 7)),
    ((3, 2), (3, 4)), ((3, 6), (3, 5)), ((3, 3), (3, 1)),
)


def flipped(index, mask, bits):
    result = 0
    for k in range(bits):
        bit = lax.rem(lax.div(index, 1 << k), 2)
        result = result + ((1 - bit) if (mask >> k) & 1 else bit) * (1 << k)
    return result


def contract(a, b, ca, cb):
    return lax.dot_general(a, b, (((ca,), (cb,)), ((), ())), preferred_element_type=F32)


def await_bytes(ref, sem):
    pltpu.make_async_copy(ref, ref, sem).wait()


def kernel(
    q_hbm, nk_hbm, nv_hbm, k_hbm, v_hbm, clen_hbm, nlen_hbm, fold_hbm, out_ref,
    qall, kbuf, vaug, s0, s1, m0, m1, oloc, r1, cp, r2, rx, fin, onew, lnew,
    nk_ref, nv_ref, stage_f, stage, kva, asm, kvg, clen_ref, nlen_ref, fold_ref,
    k_sem, v_sem, own_sem, small_sem, a_send, a_recv, kv_send, kv_recv, b_send, b_recv, g_send, g_recv,
    r1_send, r1_recv, r2_send, r2_recv, rx_send, rx_recv, r3_send, r3_recv, r3_own,
):
    c = lax.axis_index("ctx")
    t = lax.axis_index("tp")
    rollouts = k_hbm.shape[0]
    span = k_hbm.shape[1]
    slots = qall.shape[1]
    tps = stage.shape[0]
    group = ROWS // tps
    scale = 128 ** -0.5 * LOG2E
    ctx_peer = [flipped(c, j, 4) for j in range(slots)]
    tp_peer = [flipped(t, i, 3) for i in range(tps)]
    partner = ctx_peer[1]
    my_rows = pl.ds(pl.multiple_of(t * group, group), group)

    def rows_of(i):
        return pl.ds(pl.multiple_of(tp_peer[i] * group, group), group)

    def remote(src, dst, send, recv, ctx, tp):
        pltpu.make_async_remote_copy(
            src_ref=src, dst_ref=dst, send_sem=send, recv_sem=recv,
            device_id=(ctx, tp), device_id_type=MESH,
        ).start()

    barrier = pltpu.get_barrier_semaphore()
    for i in range(1, tps):
        pl.semaphore_signal(barrier, inc=1, device_id=(c, tp_peer[i]), device_id_type=MESH)
    for j in GREETED:
        pl.semaphore_signal(barrier, inc=1, device_id=(ctx_peer[j], t), device_id_type=MESH)

    small = [
        pltpu.make_async_copy(src, dst, small_sem.at[i])
        for i, (src, dst) in enumerate((
            (nk_hbm, nk_ref), (nv_hbm, nv_ref), (clen_hbm, clen_ref), (nlen_hbm, nlen_ref), (fold_hbm, fold_ref)))
    ]
    for copy in small:
        copy.start()
    own_copy = pltpu.make_async_copy(q_hbm.at[:, my_rows, :], qall.at[:, 0, my_rows, :], own_sem)
    own_copy.start()
    k_copies, v_copies = [], []
    for b in range(rollouts):
        k_copies.append(pltpu.make_async_copy(k_hbm.at[b], kbuf.at[b], k_sem.at[b]))
        v_copies.append(pltpu.make_async_copy(v_hbm.at[b], vaug.at[b, :, pl.ds(0, 128)], v_sem.at[b]))
        k_copies[b].start()
        v_copies[b].start()

    for copy in small:
        copy.wait()
    stage_f[...] = jnp.zeros_like(stage_f)
    for b in range(rollouts):
        keys_f = nk_ref[b].astype(F32)
        vals_f = nv_ref[b].astype(F32)
        for i in range(tps):
            stage_f[i, b : b + 1, :] = keys_f[i : i + 1, :]
            stage_f[i, rollouts + b : rollouts + b + 1, :] = vals_f[i : i + 1, :]
    stage[...] = stage_f[...].astype(BF16)
    kva[pl.ds(t, 1)] = stage[pl.ds(t, 1)]

    pl.semaphore_wait(barrier, tps - 1 + len(GREETED))

    def send_a(b):
        for i in range(1, tps):
            remote(q_hbm.at[b, rows_of(i), :], qall.at[b, 0, my_rows, :],
                   a_send.at[b], a_recv.at[b], c, tp_peer[i])

    def wait_a(b):
        await_bytes(qall.at[b, 0, pl.ds(0, ROWS - group), :], a_recv.at[b])

    for b in range(rollouts):
        send_a(b)
    for i in range(1, tps):
        remote(stage.at[tp_peer[i]], kva.at[t], kv_send, kv_recv, c, tp_peer[i])

    def send_b(b, *to):
        for j in to:
            remote(qall.at[b, 0], qall.at[b, j], b_send.at[b], b_recv.at[b, j], ctx_peer[j], t)

    def pass_on(*pairs):
        for b, p in pairs:
            await_bytes(qall.at[b, 2 * p], b_recv.at[b, 2 * p])
            remote(qall.at[b, 2 * p], qall.at[b, 2 * p + 1], b_send.at[b], b_recv.at[b, 2 * p + 1], partner, t)

    def wait_odd(*pairs):
        for b, p in pairs:
            await_bytes(qall.at[b, 2 * p + 1], b_recv.at[b, 2 * p + 1])

    def kv_pass_on():
        for j in range(2, slots, 2):
            await_bytes(kvg.at[j], g_recv.at[j])
            remote(kvg.at[j], kvg.at[j + 1], g_send, g_recv.at[j + 1], partner, t)

    def prepare(b):
        open_count = clen_ref[b] - fold_ref[c] * span
        for r in range(0, span, 256):
            row = lax.broadcasted_iota(jnp.int32, (256, 128), 0) + r
            is_open = row < open_count
            first = kbuf[b, 0:16, :].astype(F32)[0:1, :]
            kbuf[b, r : r + 256, :] = jnp.where(
                is_open, kbuf[b, r : r + 256, :].astype(F32), first).astype(BF16)
            vaug[b, r : r + 256, 0:128] = jnp.where(
                is_open, vaug[b, r : r + 256, 0:128].astype(F32), 0.0).astype(BF16)
            vaug[b, r : r + 256, 128:256] = jnp.where(is_open, 1.0, 0.0).astype(BF16)

    eye = (lax.broadcasted_iota(jnp.int32, (ROWS, ROWS), 0)
           == lax.broadcasted_iota(jnp.int32, (ROWS, ROWS), 1))

    def by_rollout(pairs):
        if pairs[0][0] == pairs[1][0]:
            return [(pairs[0][0], [p for _, p in pairs], slice(0, 4 * ROWS))]
        return [(b, [p], slice(2 * ROWS * i, 2 * ROWS * (i + 1))) for i, (b, p) in enumerate(pairs)]

    def score_step(pairs, s_ref, m_ref):
        for b, members, rows in by_rollout(pairs):
            queries = jnp.concatenate([qall[b, 2 * p : 2 * p + 2] for p in members], axis=0)
            queries = queries.reshape(2 * ROWS * len(members), 128)
            top = None
            for k in range(0, span, CHUNK):
                s = contract(queries, kbuf[b, k : k + CHUNK, :], 1, 1)
                s_ref[rows, k : k + CHUNK] = s
                for x in range(0, CHUNK, 128):
                    part = s[:, x : x + 128]
                    top = part if top is None else jnp.maximum(top, part)
            m_ref[rows, :] = jnp.broadcast_to(jnp.max(top, axis=1, keepdims=True) * scale, top.shape)

    def stat_rows(stat):
        high = stat.astype(BF16).astype(F32)
        middle = (stat - high).astype(BF16).astype(F32)
        low = stat - high - middle
        row = lax.broadcasted_iota(jnp.int32, (TAIL, 128), 0)
        return jnp.where(row == 0, high, jnp.where(row == 1, middle, jnp.where(row == 2, low, 0.0))).astype(BF16)

    def stat_of(rows):
        return jnp.sum(rows.astype(F32), axis=0, keepdims=True)

    def diagonal(weight):
        return jnp.where(eye, jnp.broadcast_to(weight, (ROWS, ROWS)), 0.0).astype(BF16)

    def to_row(replicated):
        return jnp.sum(jnp.where(eye, replicated, 0.0), axis=0, keepdims=True)

    def finish(total, weight, top):
        live = weight > 0.0
        safe = jnp.where(live, weight, 1.0)
        return (jnp.where(live, total / safe, 0.0), jnp.where(live, top + jnp.log2(safe), CLOSED))

    def weigh_step(pairs, s_ref, m_ref):
        for b, members, rows in by_rollout(pairs):
            top = m_ref[rows, :]
            total = None
            for k in range(0, span, CHUNK):
                parts = []
                for x in range(k, k + CHUNK, 128):
                    parts.append(jnp.exp2(s_ref[rows, x : x + 128] * scale - top).astype(BF16))
                d = contract(jnp.concatenate(parts, axis=1), vaug[b, k : k + CHUNK, :], 1, 0)
                total = d if total is None else total + d
            mean, level = finish(total[:, 0:128], total[:, 128:256], top)
            mean = mean.astype(BF16)
            for i, p in enumerate(members):
                for core in range(2):
                    at_rows = slice((2 * i + core) * ROWS, (2 * i + core + 1) * ROWS)
                    oloc[b, p, core, 0:ROWS, :] = mean[at_rows]
                    oloc[b, p, core, ROWS : ROWS + TAIL, :] = stat_rows(to_row(level[at_rows]))

    def blend(pieces, levels):
        top = functools.reduce(jnp.maximum, levels)
        weights = [jnp.exp2(level - top) for level in levels]
        total = functools.reduce(jnp.add, weights)
        share = 1.0 / total
        left = jnp.concatenate([diagonal(weight * share) for weight in weights], axis=1)
        mixed = contract(left, jnp.concatenate(pieces, axis=0), 1, 0)
        return mixed, top + jnp.log2(total)

    def chip_blend(b, p):
        mixed, level = blend(
            [oloc[b, p, 0, 0:ROWS, :], r1[b, p, 0:ROWS, :]],
            [stat_of(oloc[b, p, 0, ROWS : ROWS + TAIL, :]), stat_of(r1[b, p, ROWS : ROWS + TAIL, :])],
        )
        cp[b, p, 0:ROWS, :] = mixed.astype(BF16)
        cp[b, p, ROWS : ROWS + TAIL, :] = stat_rows(level)

    def new_part(b):
        blocks = [kvg[j, b].astype(F32) for j in range(slots)]
        keys = jnp.concatenate([x[0:8] for x in blocks], axis=0).astype(BF16)
        values = jnp.concatenate([x[8:16] for x in blocks], axis=0).astype(BF16)
        column = lax.broadcasted_iota(jnp.int32, (ROWS, ROWS), 1)
        position = lax.rem(column, tps)
        for j in range(slots):
            position = position + jnp.where(lax.div(column, tps) == j, ctx_peer[j] * tps, 0)
        row = lax.broadcasted_iota(jnp.int32, (ROWS, ROWS), 0)
        allowed = position <= c * tps + lax.div(row, group)
        s = jnp.where(allowed, contract(qall[b, 0, 0:ROWS, :], keys, 1, 1) * scale, CLOSED)
        top = jnp.max(s, axis=1, keepdims=True)
        p = jnp.exp2(s - top)
        weight = jnp.sum(p, axis=1, keepdims=True)
        mean = contract(p.astype(BF16), values, 1, 0) / weight
        onew[b] = mean.astype(BF16)
        lnew[b] = jnp.broadcast_to(
            to_row(jnp.broadcast_to(top + jnp.log2(weight), (ROWS, ROWS))), (8, 128))

    def last_blend(b):
        sources = [cp.at[b, 0]] + [r2.at[b, p] for p in range(1, slots // 2)]
        if b == rollouts - 1:
            sources += [rx.at[i] for i in range(len(LAST))]
        pieces = [x[0:ROWS, :] for x in sources] + [onew[b]]
        levels = [stat_of(x[ROWS : ROWS + TAIL, :]) for x in sources] + [lnew[b, 0:1, :]]
        mixed, _ = blend(pieces, levels)
        token = c * tps + lax.div(lax.broadcasted_iota(jnp.int32, (ROWS, 128), 0), group)
        fin[b] = jnp.where(token < nlen_ref[b], mixed, 0.0).astype(BF16)

    def send_r1(b, p):
        remote(oloc.at[b, p, 1], r1.at[b, p], r1_send.at[b], r1_recv.at[b, p], partner, t)

    def wait_r1(b, p):
        await_bytes(r1.at[b, p], r1_recv.at[b, p])

    def send_r2(b, p):
        if p:
            remote(cp.at[b, p], r2.at[b, p], r2_send.at[b], r2_recv.at[b], ctx_peer[2 * p], t)

    def send_last(pairs):
        for b, p in pairs:
            i = LAST.index(p)
            remote(oloc.at[b, p, 0], r2.at[b, p], r2_send.at[b], r2_recv.at[b], ctx_peer[2 * p], t)
            remote(oloc.at[b, p, 1], rx.at[i], rx_send, rx_recv, ctx_peer[2 * p + 1], t)

    def wait_r2(b):
        await_bytes(r2.at[b, pl.ds(1, slots // 2 - 1)], r2_recv.at[b])

    def send_r3(b):
        for i in range(1, tps):
            remote(fin.at[b, rows_of(i), :], out_ref.at[b, my_rows, :], r3_send, r3_recv, c, tp_peer[i])

    for b in range(rollouts):
        k_copies[b].wait()
        v_copies[b].wait()
        prepare(b)
    own_copy.wait()
    for b in range(rollouts):
        wait_a(b)
        send_b(b, 1)
    send_b(0, *NEAR)
    bufs = ((s0, m0), (s1, m1))
    wait_odd(*ORDER[0])
    score_step(ORDER[0], *bufs[0])

    def kv_start():
        await_bytes(kva.at[pl.ds(0, tps - 1)], kv_recv)
        for i in range(tps):
            block = kva[i].astype(F32)
            for b in range(rollouts):
                asm[b, i : i + 1, :] = block[b : b + 1, :]
                asm[b, tps + i : tps + i + 1, :] = block[rollouts + b : rollouts + b + 1, :]
        kvg[0] = asm[...].astype(BF16)
        for j in NEAR + FAR + (1,):
            remote(kvg.at[0], kvg.at[j], g_send, g_recv.at[j], ctx_peer[j], t)

    def kv_end():
        for j in range(1, slots, 2):
            await_bytes(kvg.at[j], g_recv.at[j])

    def finish_rollout(b):
        last_blend(b)
        send_r3(b)

    count = len(ORDER)
    before, beside, after = ({n: [] for n in range(count + 2)} for _ in range(3))

    def at(when, step, what, *args):
        when[step].append((what, args))

    at(before, 0, send_b, 0, *FAR)
    at(before, 1, pass_on, (0, 1), (0, 3), (0, 4))
    at(before, 1, send_b, 1, *NEAR, *FAR)
    at(before, 2, pass_on, (0, 2))
    at(before, 3, pass_on, (0, 5), (0, 6), (0, 7), (1, 1))
    at(before, 4, pass_on, (1, 3), (1, 4))
    at(before, 5, pass_on, (1, 2), (1, 5))
    at(before, 6, pass_on, (1, 6), (1, 7))
    for n in range(7, count - 2):
        at(before, n, pass_on, *ORDER[n + 2])
    for n in range(count - 1):
        at(before, n, wait_odd, *ORDER[n + 1])
    at(before, 2, kv_start)
    at(before, 3, send_b, 2, *NEAR, *FAR)
    at(before, 6, send_b, 3, *NEAR, *FAR)
    at(before, 8, kv_pass_on)
    at(before, 10, kv_end)
    for n, pairs in enumerate(ORDER[:-2]):
        for pair in pairs:
            at(after, n, send_r1, *pair)
    for n, pairs in enumerate(ORDER[:-2]):
        later = min(n + 2, count)
        for pair in pairs:
            at(before, later, wait_r1, *pair)
            at(beside, later, chip_blend, *pair)
            at(after, later, send_r2, *pair)
    for n in (count - 2, count - 1):
        at(after, n, send_last, ORDER[n])
    for b in range(rollouts):
        at(beside, 10 + b, new_part, b)
    for b, step in ((0, 12), (1, 14)):
        at(before, step, wait_r2, b)
        at(beside, step, last_blend, b)
        at(after, step, send_r3, b)

    for n, pairs in enumerate(ORDER):
        for what, args in before[n]:
            what(*args)
        if n + 1 < count:
            score_step(ORDER[n + 1], *bufs[(n + 1) % 2])
        weigh_step(pairs, *bufs[n % 2])
        for what, args in beside[n] + after[n]:
            what(*args)
    for what, args in before[count] + beside[count] + after[count]:
        what(*args)
    wait_r2(2)
    finish_rollout(2)
    wait_r2(3)
    await_bytes(rx, rx_recv)
    finish_rollout(3)
    keep = pltpu.make_async_copy(fin.at[:, my_rows, :], out_ref.at[:, my_rows, :], r3_own)
    keep.start()

    for b in range(rollouts):
        await_bytes(qall.at[b, 0, pl.ds(0, ROWS - group), :], a_send.at[b])
        await_bytes(qall.at[b, pl.ds(0, slots - 1)], b_send.at[b])
        await_bytes(r1.at[b, pl.ds(0, slots // 2 - (len(LAST) if b == rollouts - 1 else 0))], r1_send.at[b])
        await_bytes(r2.at[b, pl.ds(1, slots // 2 - 1)], r2_send.at[b])
    await_bytes(kva.at[pl.ds(0, tps - 1)], kv_send)
    await_bytes(rx, rx_send)
    await_bytes(kvg.at[pl.ds(0, slots - 1)], g_send)
    await_bytes(fin.at[:, pl.ds(0, ROWS - group), :], r3_send)
    await_bytes(fin.at[:, pl.ds(0, ROWS - group), :], r3_recv)
    keep.wait()


def shards(queries, new_keys, turn_value_rows, cache_keys, cache_values, cached_len, new_len, fold):
    rollouts, span = cache_keys.shape[0], cache_keys.shape[1]
    slots, tps = lax.axis_size("ctx"), lax.axis_size("tp")
    any_space = pl.BlockSpec(memory_space=pl.ANY)
    dma = pltpu.SemaphoreType.DMA
    block = (ROWS + TAIL, 128)
    out = pl.pallas_call(
        kernel,
        out_shape=jax.ShapeDtypeStruct((rollouts, 128, 128), BF16),
        in_specs=[any_space] * 8,
        out_specs=any_space,
        scratch_shapes=[
            pltpu.VMEM((rollouts, slots, ROWS, 128), BF16),
            pltpu.VMEM((rollouts, span, 128), BF16),
            pltpu.VMEM((rollouts, span, 256), BF16),
            pltpu.VMEM((4 * ROWS, span), F32),
            pltpu.VMEM((4 * ROWS, span), F32),
            pltpu.VMEM((4 * ROWS, 128), F32),
            pltpu.VMEM((4 * ROWS, 128), F32),
            pltpu.VMEM((rollouts, slots // 2, 2) + block, BF16),
            pltpu.VMEM((rollouts, slots // 2) + block, BF16),
            pltpu.VMEM((rollouts, slots // 2) + block, BF16),
            pltpu.VMEM((rollouts, slots // 2) + block, BF16),
            pltpu.VMEM((len(LAST),) + block, BF16),
            pltpu.VMEM((rollouts, ROWS, 128), BF16),
            pltpu.VMEM((rollouts, ROWS, 128), BF16),
            pltpu.VMEM((rollouts, 8, 128), F32),
            pltpu.VMEM((rollouts, tps, 128), BF16),
            pltpu.VMEM((rollouts, tps, 128), BF16),
            pltpu.VMEM((tps, TAIL, 128), F32),
            pltpu.VMEM((tps, TAIL, 128), BF16),
            pltpu.VMEM((tps, TAIL, 128), BF16),
            pltpu.VMEM((rollouts, TAIL, 128), F32),
            pltpu.VMEM((slots, rollouts, TAIL, 128), BF16),
            pltpu.SMEM((rollouts,), jnp.int32), pltpu.SMEM((rollouts,), jnp.int32),
            pltpu.SMEM((slots,), jnp.int32),
            dma((rollouts,)), dma((rollouts,)), dma, dma((5,)),
            dma((rollouts,)), dma((rollouts,)),
            dma, dma,
            dma((rollouts,)), dma((rollouts, slots)),
            dma, dma((slots,)),
            dma((rollouts,)), dma((rollouts, slots // 2)),
            dma((rollouts,)), dma((rollouts,)),
            dma, dma,
            dma, dma, dma,
        ],
        compiler_params=pltpu.CompilerParams(
            collective_id=0, has_side_effects=True, vmem_limit_bytes=56 << 20),
        name="turn_attention",
    )(
        queries[:, 0], new_keys[:, 0], turn_value_rows[:, 0],
        cache_keys[:, :, 0], cache_values[:, :, 0], cached_len, new_len, fold,
    )
    return out[:, None]


def solution(mesh):
    in_specs = (
        P(None, ("ctx", "tp"), None, None),
        P(None, ("ctx", "tp"), None, None),
        P(None, ("ctx", "tp"), None, None),
        P(None, "ctx", "tp", None),
        P(None, "ctx", "tp", None),
        P(),
        P(),
        P(),
    )
    out_specs = P(None, ("ctx", "tp"), None, None)
    return jax.shard_map(shards, mesh=mesh, in_specs=in_specs, out_specs=out_specs, check_vma=False)
```
